128 devices in a mesh: dp: 8 (over x, core), seq: 16 (over y, z).
Axes of the slice: x: 4, y: 4, z: 4, core: 2. Of those that a mesh axis runs over, the one named last changes fastest.
Arguments:
- inputs: float32 [16, 1024, 512], P('dp', 'seq'), may hold values from -6 to 6
- cotangent: float32 [16, 1024, 512], P('dp', 'seq'), may hold values from -6 to 6
- lengths: int32 [16], P('dp'), may hold values from 1 to 1024, as said below
- gain_first: bfloat16 [512], P(('dp', 'seq')), may hold values from 0.099609375 to 1.8984375
- proj_in: bfloat16 [512, 1024], P(('dp', 'seq')), may hold values from -0.25 to 0.25
- sub_kernels: bfloat16 [5, 32, 512], P(None, None, ('dp', 'seq')), may hold values from -6 to 6
- skip_gain: bfloat16 [512], P(('dp', 'seq')), may hold values from -3 to 3
- proj_out: bfloat16 [512, 512], P(('dp', 'seq')), may hold values from -0.5 to 0.5
- gain_second: bfloat16 [512], P(('dp', 'seq')), may hold values from 0.099609375 to 1.8984375
- mlp_up: bfloat16 [512, 2048], P(('dp', 'seq')), may hold values from -0.25 to 0.25
- mlp_down: bfloat16 [2048, 512], P(('dp', 'seq')), may hold values from -0.1875 to 0.1875
Outputs:
- outputs: float32 [16, 1024, 512], P('dp', 'seq')
- grad_inputs: float32 [16, 1024, 512], P('dp', 'seq')
- grad_gain_first: float32 [512], P(('dp', 'seq'))
- grad_proj_in: float32 [512, 1024], P(('dp', 'seq'))
- grad_sub_kernels: float32 [5, 32, 512], P(None, None, ('dp', 'seq'))
- grad_skip_gain: float32 [512], P(('dp', 'seq'))
- grad_proj_out: float32 [512, 512], P(('dp', 'seq'))
- grad_gain_second: float32 [512], P(('dp', 'seq'))
- grad_mlp_up: float32 [512, 2048], P(('dp', 'seq'))
- grad_mlp_down: float32 [2048, 512], P(('dp', 'seq'))
The draws below stay inside these ranges and needn't reach their ends.
Inputs may be any that keep to these rules, and one draw needn't show every extreme that they name: `lengths`: each aligned group of 2 sequences (those of one index of dp) holds one sequence of length 1024; positions at or past a sequence's length are padding.
All inputs are finite; a program needn't handle non-finite values.
Results may differ from the reference program's by a relative error of at most 0.013.
Values may be sent and summed in bfloat16 or wider, within the bound.
A program may use at most 128 MiB of HBM per device.

```python
import jax
import jax.numpy as jnp
from jax import lax

D = 512
FF = 2048
SUBTAPS = 32
NSUB = 5
SEQS = 2
SLOT = 1024
BATCH = 16


def draw_lengths(key, part):
    key = jax.random.fold_in(key, 17)
    length_key, pick_key = jax.random.split(key)
    drawn = jax.random.randint(length_key, (BATCH,), 1, SLOT + 1)
    chosen = jax.random.randint(pick_key, (BATCH // SEQS,), 0, SEQS)
    longest = (jnp.arange(SEQS)[None, :] == chosen[:, None]).reshape(BATCH)
    return jnp.where(longest, SLOT, drawn).astype(jnp.int32)


def block_levels(key, extent, shards, smallest, top_value):
    loudness = 1.0
    for axis_at, shards_of in shards:
        steps = jax.random.uniform(jax.random.fold_in(jax.random.fold_in(key, 6), axis_at), (shards_of,), jnp.float32, smallest / len(shards), top_value / len(shards))
        loudness = loudness * jnp.repeat(jnp.exp(steps), extent[axis_at] // shards_of).reshape((-1,) + (1,) * (len(extent) - 1 - axis_at))
    return loudness


def noise(rng, shape, width, bound, cuts=(), held_as=jnp.bfloat16):
    array = jax.random.normal(rng, shape, jnp.float32) * width
    if len(cuts) > 0:
        array = block_levels(rng, shape, cuts, -0.22, 0.18) * array
    return jnp.clip(array, min=-bound, max=bound).astype(held_as)


def setup_inputs(seed: int = 0) -> dict:
    seeds = jax.random.split(jax.random.key(seed), 12)
    inputs = noise(seeds[0], (BATCH, SLOT, D), 1.0, 6.0, ((0, 8), (1, 16)), jnp.float32)
    cotangent = noise(seeds[1], (BATCH, SLOT, D), 1.0, 6.0, ((0, 8), (1, 16)), jnp.float32)
    lengths = draw_lengths(jax.random.fold_in(seeds[11], 71), 0)
    gain_first = jnp.clip(1.0 + 0.18 * jax.random.normal(seeds[3], (D,), jnp.float32), 0.099609375, 1.8984375).astype(jnp.bfloat16)
    proj_in = noise(seeds[4], (D, 2 * D), D ** -0.5, 0.25, ((0, 128),))
    sub_kernels = noise(seeds[5], (NSUB, SUBTAPS, D), 1.0, 6.0, ((2, 128),))
    skip_gain = noise(seeds[6], (D,), 0.5, 3.0, ((0, 128),))
    proj_out = noise(seeds[7], (D, D), (D // 4) ** -0.5, 0.5, ((0, 128),))
    gain_second = jnp.clip(1.0 + 0.18 * jax.random.normal(seeds[8], (D,), jnp.float32), 0.099609375, 1.8984375).astype(jnp.bfloat16)
    mlp_up = noise(seeds[9], (D, FF), D ** -0.5, 0.25, ((0, 128),))
    mlp_down = noise(seeds[10], (FF, D), (FF // 2) ** -0.5, 0.1875, ((0, 128),))
    return dict(inputs=inputs, cotangent=cotangent, lengths=lengths, gain_first=gain_first, proj_in=proj_in, sub_kernels=sub_kernels, skip_gain=skip_gain, proj_out=proj_out, gain_second=gain_second, mlp_up=mlp_up, mlp_down=mlp_down)


EPSILON = 1e-05

@jax.custom_vjp
def low(v):
    return lax.optimization_barrier(v.astype(jnp.bfloat16)).astype(jnp.float32)

@jax.custom_vjp
def low_back(v):
    return v

def low_keep(v):
    return (low(v), None)

def low_pass(kept, grad):
    return (grad,)

def back_keep(v):
    return (v, None)

def back_low(kept, grad):
    return (low(grad),)
low.defvjp(low_keep, low_pass)
low_back.defvjp(back_keep, back_low)

def layer_norm(values, gain_vec):
    centered = values - lax.optimization_barrier(jnp.mean(values, axis=-1, keepdims=True))
    variance = lax.optimization_barrier(jnp.mean(centered * centered, axis=-1, keepdims=True))
    return centered * lax.rsqrt(variance + EPSILON) * gain_vec

def build_kernel(sub_taps, length):
    pieces = []
    for octave in range(sub_taps.shape[0]):
        pieces.append(jnp.repeat(sub_taps[octave], 2 ** octave, axis=0) * 0.5 ** octave)
    kernel = jnp.concatenate(pieces, axis=0)
    kernel = kernel * lax.rsqrt(lax.optimization_barrier(jnp.sum(kernel * kernel, axis=0, keepdims=True)) + EPSILON)
    if kernel.shape[0] >= length:
        return kernel[:length]
    return jnp.pad(kernel, ((0, length - kernel.shape[0]), (0, 0)))

def matmul_rows(left, right):
    return jnp.einsum('bsd,de->bse', left, right, precision=lax.Precision.HIGHEST)

def causal_conv(signal, kernel):
    length = signal.shape[1]
    spectrum = jnp.fft.rfft(signal, n=2 * length, axis=1) * jnp.fft.rfft(kernel, n=2 * length, axis=0)[None]
    return jnp.fft.irfft(spectrum, n=2 * length, axis=1)[:, :length]

def exact_gelu(values):
    return jax.nn.gelu(values, approximate=False)

def reference(inputs, cotangent, lengths, gain_first, proj_in, sub_kernels, skip_gain, proj_out, gain_second, mlp_up, mlp_down):
    positions = jnp.arange(SLOT, dtype=jnp.int32)
    row_mask = (positions[None, :] < lengths[:, None]).astype(jnp.float32)[:, :, None]

    def forward(source, gain_one, w_in, sub_taps, skip_vec, w_out, gain_two, w_up, w_down):
        normed = layer_norm(source, gain_one)
        projected = low_back(matmul_rows(low(normed), w_in))
        values = projected[..., :D]
        gates = projected[..., D:]
        kernel = low(build_kernel(sub_taps, SLOT))
        conv = low_back(causal_conv(low(values), kernel))
        mixed = conv + skip_vec * values
        branch_out = low_back(matmul_rows(low(mixed * exact_gelu(gates)), w_out))
        hidden = source + row_mask * branch_out
        normed_two = layer_norm(hidden, gain_two)
        up_proj = low_back(matmul_rows(low(normed_two), w_up))
        mlp_out = low_back(matmul_rows(low(exact_gelu(up_proj)), w_down))
        return hidden + row_mask * mlp_out
    outputs, pullback = jax.vjp(forward, inputs, gain_first.astype(jnp.float32), proj_in.astype(jnp.float32), sub_kernels.astype(jnp.float32), skip_gain.astype(jnp.float32), proj_out.astype(jnp.float32), gain_second.astype(jnp.float32), mlp_up.astype(jnp.float32), mlp_down.astype(jnp.float32))
    grads = pullback(cotangent)
    return (outputs, grads[0], grads[1], grads[2], grads[3], grads[4], grads[5], grads[6], grads[7], grads[8])
```

```python
import math

import jax
import jax.numpy as jnp
import ml_dtypes
import numpy as np
from jax import lax
from jax.experimental import pallas as pl
from jax.experimental.pallas import tpu as pltpu
from jax.sharding import PartitionSpec as P

EPSILON = 1e-05
D = 512
FF = 2048
SLOT = 1024
NSUB = 5
SUBTAPS = 32
TAPS = NSUB * SUBTAPS
F32 = jnp.float32
BF16 = jnp.bfloat16
MESH = pl.DeviceIdType.MESH

VAL, EXT, UPA, GAT, OUT, UPB, END, WIDE = 0, 512, 768, 1792, 2304, 2816, 3840, 4096
XE, XU, YG, YU = (VAL, UPA), (UPA, GAT), (GAT, UPB), (UPB, END)


def transforms():
    place = np.arange(SLOT)
    angle = 2 * np.pi * ((2 * place[:, None] + 1) * place[None, :] % (4 * SLOT)) / (4 * SLOT)
    forward = np.concatenate([np.cos(angle), -np.sin(angle)], axis=0)
    inverse = forward.T / SLOT
    repeat = np.zeros((SLOT, 256))
    first = 0
    for octave in range(NSUB):
        for tap in range(SUBTAPS):
            repeat[first : first + 2**octave, octave * SUBTAPS + tap] = 0.5**octave
            first += 2**octave
    half = np.stack([inverse[:512], inverse[512:]])
    return tuple(a.astype(ml_dtypes.bfloat16) for a in (forward, half, forward @ repeat))


def nn(a, b):
    return lax.dot_general(a, b, (((1,), (0,)), ((), ())), preferred_element_type=F32)


def nt(a, b):
    return lax.dot_general(a, b, (((1,), (1,)), ((), ())), preferred_element_type=F32)


def tn(a, b):
    return lax.dot_general(a, b, (((0,), (0,)), ((), ())), preferred_element_type=F32)


def gelu_parts(v):
    cdf = 0.5 * (1.0 + lax.erf(v * math.sqrt(0.5)))
    slope = cdf + v * (jnp.exp(-0.5 * v * v) * (1.0 / math.sqrt(2 * math.pi)))
    return v * cdf, slope


def swap_matrix():
    row = lax.broadcasted_iota(jnp.int32, (64, 64), 0)
    col = lax.broadcasted_iota(jnp.int32, (64, 64), 1)
    source = ((row >> 2) & 3) * 16 + (row >> 4) * 4 + (row & 3)
    return jnp.where(col == source, 1.0, 0.0).astype(BF16)


def fused(
    x_ref, cot_ref, len_ref, pack_ref, down_ref, dft_hbm, inv_hbm, rep_hbm,
    out_ref, gin_ref, gpack_ref, gdown_ref,
    zin, wb, wd, dft, inv, rep,
    xh1, inv1, nlow, val, gated, dgel, mixed, bi, hid, xh2, n2l, gmo, gact, act, gup, ghid, gb, ggate, prods,
    vsend, vin, ysend, cin, gsend, gvin, csend, gcin, spec_v, spec_k, spec_g, spec_y,
    acc, csw, crw, s2, r2, acc2, s3, r3, tail,
    accd, csd, crd, s2d, r2d, acc2d, s3d, r3d, acc3d, s4d, r4d, s4, r4,
    send_sem, recv_sem, local_sem,
):
    dp, j = lax.axis_index("dp"), lax.axis_index("seq")
    x, c = dp // 2, dp % 2
    y, z = j // 4, j % 4
    half, pair = j % 2, j // 2
    group = pair % 4

    def turn(v, by):
        return lax.rem(v + by, 4)

    def x_at(v):
        return (v * 2 + c, j)

    def y_at(v):
        return (dp, v * 4 + z)

    def z_at(v):
        return (dp, y * 4 + v)

    sibling = (x * 2 + 1 - c, j)

    barrier = pltpu.get_barrier_semaphore()
    partners = [sibling] + [x_at(turn(x, i)) for i in (1, 2, 3)]
    partners += [(dp, lax.rem(j + i, 16)) for i in range(1, 16)]
    for partner in partners:
        pl.semaphore_signal(barrier, inc=1, device_id=partner, device_id_type=MESH)

    loads = [
        pltpu.make_async_copy(rep_hbm, rep, local_sem.at[0]),
        pltpu.make_async_copy(dft_hbm, dft, local_sem.at[1]),
        pltpu.make_async_copy(inv_hbm.at[half], inv, local_sem.at[2]),
    ]
    for load in loads:
        load.start()

    zin[z] = pack_ref[...]
    wd[x, c, y, z] = down_ref[...]

    pl.semaphore_wait(barrier, len(partners))

    started = []

    def push(src, dst, device):
        at = len(started)
        copy = pltpu.make_async_remote_copy(
            src_ref=src,
            dst_ref=dst,
            send_sem=send_sem.at[at],
            recv_sem=recv_sem.at[at],
            device_id=device,
            device_id_type=MESH,
        )
        copy.start()
        started.append(copy)
        return copy

    def ring(me, at, src, dst):
        return [push(src(turn(me, i)), dst(i), at(turn(me, i))) for i in (1, 2, 3)]

    def arrived(copies):
        for copy in copies:
            copy.wait_recv()

    def same(me, at, ref):
        return ring(me, at, lambda to: ref, lambda i: ref)

    got_z = same(z, z_at, zin.at[z])
    got_dx = same(x, x_at, wd.at[x, c, y, z])

    source = x_ref[...]
    centered = source - jnp.mean(source, axis=1, keepdims=True)
    inv_one = lax.rsqrt(jnp.mean(centered * centered, axis=1, keepdims=True) + EPSILON)
    inv1[...] = inv_one
    xh1[...] = centered * inv_one

    row = lax.broadcasted_iota(jnp.int32, (128, 1), 0)
    limit = jnp.where(row < 64, len_ref[0], len_ref[1])
    mask = jnp.where((row & 63) + j * 64 < limit, 1.0, 0.0)

    swap = swap_matrix()
    arrived(got_z)
    rows = nn(swap, zin[...].reshape(64, 1024)).astype(BF16)
    for u in range(4):
        wb[x, c, y, :, 1024 * u : 1024 * (u + 1)] = rows[16 * u : 16 * u + 16]

    def cols(ends):
        return pl.ds(ends[0], ends[1] - ends[0])

    def first_x(p):
        return same(y, y_at, wb.at[x, c, y, :, cols(p)])

    def first_y(p):
        return same(x, x_at, wb.at[x, c, y, :, cols(p)])

    def bulk_x(p):
        return same(x, x_at, wb.at[x, c, :, :, cols(p)])

    def bulk_y(p):
        return same(y, y_at, wb.at[:, c, y, :, cols(p)])

    def to_sibling(p):
        ref = wb.at[:, c, :, :, cols(p)]
        return [push(ref, ref, sibling)]

    got_xe, got_yg, got_xu, got_yu = first_x(XE), first_y(YG), first_x(XU), first_y(YU)
    arrived(got_dx)
    got_dy = same(y, y_at, wd.at[:, c, y, z])
    arrived(got_xe)
    got_xe = bulk_x(XE)
    arrived(got_yg)
    got_yg = bulk_y(YG)
    arrived(got_dy)
    got_dz = same(z, z_at, wd.at[:, c, :, z])
    arrived(got_xu)
    arrived(got_yu)
    arrived(got_xe)
    got_xe = to_sibling(XE)
    arrived(got_yg)
    got_yg = to_sibling(YG)
    got_xu = bulk_x(XU)
    got_yu = bulk_y(YU)

    def weight(first, width):
        return wb[:, :, :, :, first : first + width].reshape(512, width)

    arrived(got_xe)
    pick = jnp.where(
        lax.broadcasted_iota(jnp.int32, (8, 128), 1)
        == lax.broadcasted_iota(jnp.int32, (8, 128), 0) + (TAPS - 128),
        1.0,
        0.0,
    ).astype(BF16)
    gains = nt(pick, weight(EXT + 128, 128))
    gain_one, gain_two, skip = gains[0:1], gains[1:2], gains[2:3]
    nlow[...] = (xh1[...] * gain_one).astype(BF16)
    values = nn(nlow[...], weight(VAL, 512))
    val[...] = values
    low = values.astype(BF16)
    for b in range(2):
        for g in range(4):
            vsend[4 * b + g] = low[64 * b : 64 * b + 64, 128 * g : 128 * g + 128]

    def scatter(src, dst):
        copies = []
        for i in range(1, 16):
            to = lax.rem(j + i, 16)
            copies.append(push(src.at[to // 2], dst.at[j], (dp, to)))
        dst[j] = src[pair]
        return copies

    def give_back(src, dst):
        base = len(started)
        copies = []
        for i in range(8):
            to = 8 * half + i
            copy = pltpu.make_async_remote_copy(
                src_ref=src.at[i],
                dst_ref=dst.at[pair],
                send_sem=send_sem.at[base + i],
                recv_sem=recv_sem.at[base + pair],
                device_id=(dp, to),
                device_id_type=MESH,
            )

            @pl.when(to != j)
            def _(copy=copy):
                copy.start()

            @pl.when(to == j)
            def _(i=i):
                dst[pair] = src[i]

            copies.append((copy, to))
            started.append(None)
        receipts = []
        for q in range(8):
            receipt = pltpu.make_async_remote_copy(
                src_ref=src.at[q],
                dst_ref=dst.at[q],
                send_sem=send_sem.at[base + q],
                recv_sem=recv_sem.at[base + q],
                device_id=sibling,
                device_id_type=MESH,
            )
            receipts.append((receipt, 2 * q + j // 8))
        return copies, receipts

    def taken_back(receipts):
        for receipt, sender in receipts:

            @pl.when(sender != j)
            def _(receipt=receipt):
                receipt.wait_recv()

    def sent_back(copies):
        for copy, to in copies:

            @pl.when(to != j)
            def _(copy=copy):
                copy.wait_send()

    got_v = scatter(vsend, vin)

    arrived(got_yg)
    gates = nn(nlow[...], weight(GAT, 512))
    gated[...], dgel[...] = gelu_parts(gates)

    taps = wb[group, :, :, :, EXT:UPA].reshape(128, 256)
    lane = lax.broadcasted_iota(jnp.int32, (128, 256), 1)
    share = jnp.where(lane < TAPS, 1.0 / (1 << (lane >> 5)).astype(F32), 0.0)
    squares = taps.astype(F32) * taps.astype(F32) * share
    high = squares.astype(BF16)
    rest = (squares - high.astype(F32)).astype(BF16)
    ones = jnp.ones((8, 256), BF16)
    norm = lax.rsqrt((nt(ones, high) + nt(ones, rest))[0:1] + EPSILON)
    loads[0].wait()
    for i in range(4):
        part = pl.ds(512 * i, 512)
        spec_k[part, :] = nt(rep[part, :], taps) * norm

    def spectrum(src, dst):
        signal = src[...].reshape(SLOT, 128)

        def step(i, carry):
            part = pl.ds(pl.multiple_of(i * 256, 256), 256)
            dst[part, :] = nn(dft[part, :], signal)
            return carry

        lax.fori_loop(0, 8, step, 0)

    def back(dst):
        def step(i, carry):
            rows_of = inv[pl.ds(pl.multiple_of(i * 256, 256), 256), :]
            dst[pl.ds(i * 4, 4)] = nn(rows_of, spec_y[...]).astype(BF16).reshape(4, 64, 128)
            return carry

        lax.fori_loop(0, 2, step, 0)

    loads[1].wait()
    loads[2].wait()
    arrived(got_v)
    spectrum(vin, spec_v)
    for i in range(4):
        re, im = pl.ds(256 * i, 256), pl.ds(SLOT + 256 * i, 256)
        kr, ki, vr, vi = spec_k[re, :], spec_k[im, :], spec_v[re, :], spec_v[im, :]
        spec_y[re, :] = (kr * vr - ki * vi).astype(BF16)
        spec_y[im, :] = (kr * vi + ki * vr).astype(BF16)
    back(ysend)
    sent_c, got_c = give_back(ysend, cin)

    arrived(got_xu)
    got_xu = to_sibling(XU)
    arrived(got_yu)
    got_yu = to_sibling(YU)
    arrived(got_dz)
    got_dc = [push(wd.at[:, c], wd.at[:, c], sibling)]
    gmo[...] = (cot_ref[...] * mask).astype(BF16)
    arrived(got_xu)
    arrived(got_yu)
    arrived(got_dc)
    for f in range(4):
        gact[:, 512 * f : 512 * f + 512] = nt(gmo[...], wd[f].reshape(512, 512))

    def whole(ref):
        lines = [jnp.concatenate([ref[4 * b + g] for g in range(4)], axis=1) for b in range(2)]
        return jnp.concatenate(lines, axis=0).astype(F32)

    taken_back(got_c)
    mixed[...] = whole(cin) + skip * val[...]
    bi[...] = (mixed[...] * gated[...]).astype(BF16)
    hidden = x_ref[...] + mask * nn(bi[...], weight(OUT, 512))
    hid[...] = hidden
    centered = hidden - jnp.mean(hidden, axis=1, keepdims=True)
    inv_two = lax.rsqrt(jnp.mean(centered * centered, axis=1, keepdims=True) + EPSILON)
    xh2[...] = centered * inv_two
    n2l[...] = (xh2[...] * gain_two).astype(BF16)
    up_at = (UPA, UPA + 512, UPB, UPB + 512)
    grad_n2 = jnp.zeros((128, 512), F32)
    for f in range(4):
        part = slice(512 * f, 512 * f + 512)
        w_up = weight(up_at[f], 512)
        gelu, slope = gelu_parts(nn(n2l[...], w_up))
        act[:, part] = gelu.astype(BF16)
        gup[:, part] = (gact[:, part] * slope).astype(BF16)
        grad_n2 = grad_n2 + nt(gup[:, part], w_up)
    weighted = gain_two * grad_n2
    mean_one = jnp.mean(weighted, axis=1, keepdims=True)
    mean_two = jnp.mean(weighted * xh2[...], axis=1, keepdims=True)
    grad_hidden = cot_ref[...] + (weighted - mean_one - xh2[...] * mean_two) * inv_two
    ghid[...] = grad_hidden
    gb[...] = (mask * grad_hidden).astype(BF16)
    grad_bi = nt(gb[...], weight(OUT, 512))
    grad_mixed = grad_bi * gated[...]
    low = grad_mixed.astype(BF16)
    for b in range(2):
        for g in range(4):
            gsend[4 * b + g] = low[64 * b : 64 * b + 64, 128 * g : 128 * g + 128]
    got_g = scatter(gsend, gvin)

    prods[0:128] = (grad_n2 * xh2[...]).astype(BF16)
    prods[128:256] = (grad_mixed * val[...]).astype(BF16)
    ggate[...] = (grad_bi * mixed[...] * dgel[...]).astype(BF16)
    val[...] = skip * grad_mixed

    mine = c == 0

    def split(grad, first, width):
        grad = grad.reshape(4, 2, 4, 16, width)
        at = slice(first, first + width)
        acc[:, :, :, at] = jnp.where(mine, grad[:, 0], grad[:, 1])
        csw[:, :, :, at] = jnp.where(mine, grad[:, 1], grad[:, 0]).astype(BF16)

    def swap_cores(p):
        return [push(csw.at[:, :, :, cols(p)], crw.at[:, :, :, cols(p)], sibling)]

    split(tn(n2l[...], gup[:, 0:512]), UPA, 512)
    split(tn(n2l[...], gup[:, 512:1024]), UPA + 512, 512)
    rs_xu = swap_cores(XU)
    split(tn(n2l[...], gup[:, 1024:1536]), UPB, 512)
    split(tn(n2l[...], gup[:, 1536:2048]), UPB + 512, 512)
    rs_yu = swap_cores(YU)
    for f in range(4):
        grad = tn(act[:, 512 * f : 512 * f + 512], gmo[...]).reshape(2, 4, 4, 16, 512)
        accd[f] = jnp.where(mine, grad[0], grad[1])
        csd[f] = jnp.where(mine, grad[1], grad[0]).astype(BF16)
    rs_d = [push(csd, crd, sibling)]
    split(tn(nlow[...], ggate[...]), GAT, 512)
    split(tn(bi[...], gb[...]), OUT, 512)
    rs_yg = swap_cores(YG)

    def reduce_bulk_x(p, got):
        at = slice(*p)
        arrived(got)
        for k in range(4):
            total = acc[k, :, :, at] + crw[k, :, :, at].astype(F32)
            acc[k, :, :, at] = total
            s2[k, :, :, at] = total.astype(BF16)
        return ring(
            x, x_at, lambda to: s2.at[to, :, :, cols(p)], lambda i: r2.at[i - 1, :, :, cols(p)]
        )

    def reduce_bulk_y(p, got):
        at = slice(*p)
        arrived(got)
        for k in range(4):
            total = acc[k, :, :, at] + crw[k, :, :, at].astype(F32)
            acc[k, :, :, at] = total
            s2[k, :, :, at] = total.astype(BF16)
        return ring(
            y, y_at, lambda to: s2.at[:, to, :, cols(p)], lambda i: r2.at[i - 1, :, :, cols(p)]
        )

    def reduce_next(p, got, own, me, at_device):
        at = slice(*p)
        arrived(got)
        total = own
        for k in range(3):
            total = total + r2[k, :, :, at].astype(F32)
        acc2[:, :, at] = total
        s3[:, :, at] = total.astype(BF16)
        return ring(
            me, at_device, lambda to: s3.at[to, :, cols(p)], lambda i: r3.at[i - 1, :, cols(p)]
        )

    def reduce_next_x(p, got):
        return reduce_next(p, got, acc[x, :, :, slice(*p)], y, y_at)

    def reduce_next_y(p, got):
        return reduce_next(p, got, acc[:, y, :, slice(*p)], x, x_at)

    def reduce_last(p, got, me):
        at = slice(*p)
        arrived(got)
        total = acc2[me, :, at]
        for k in range(3):
            total = total + r3[k, :, at].astype(F32)
        tail[:, at] = total

    rs_xu = reduce_bulk_x(XU, rs_xu)
    rs_yu = reduce_bulk_y(YU, rs_yu)
    arrived(rs_d)
    for k in range(4):
        total = accd[k] + crd[k].astype(F32)
        accd[k] = total
        s2d[k] = total.astype(BF16)
    rs_d = ring(z, z_at, lambda to: s2d.at[:, :, to], lambda i: r2d.at[i - 1])

    mlp_out = jnp.zeros((128, 512), F32)
    for f in range(4):
        mlp_out = mlp_out + nn(act[:, 512 * f : 512 * f + 512], wd[f].reshape(512, 512))
    out_ref[...] = hid[...] + mask * mlp_out

    arrived(got_g)
    spectrum(gvin, spec_g)
    for i in range(4):
        re, im = pl.ds(256 * i, 256), pl.ds(SLOT + 256 * i, 256)
        kr, ki, gr, gi = spec_k[re, :], spec_k[im, :], spec_g[re, :], spec_g[im, :]
        spec_y[re, :] = (kr * gr + ki * gi).astype(BF16)
        spec_y[im, :] = (kr * gi - ki * gr).astype(BF16)
    back(csend)
    sent_g, got_gc = give_back(csend, gcin)

    rs_yg = reduce_bulk_y(YG, rs_yg)

    re = pl.ds(pl.multiple_of(half * 512, 512), 512)
    im = pl.ds(pl.multiple_of(half * 512 + SLOT, 512), 512)
    vr, vi, gr, gi = spec_v[re, :], spec_v[im, :], spec_g[re, :], spec_g[im, :]
    tap_grad = tn((vr * gr + vi * gi).astype(BF16), rep[re, :])
    tap_grad = (tap_grad + tn((vr * gi - vi * gr).astype(BF16), rep[im, :])) * (1.0 / SLOT)

    rs_xu = reduce_next_x(XU, rs_xu)
    rs_yu = reduce_next_y(YU, rs_yu)

    taken_back(got_gc)
    grad_val = (whole(gcin) + val[...]).astype(BF16)
    grad_normed = nt(grad_val, weight(VAL, 512)) + nt(ggate[...], weight(GAT, 512))
    prods[256:384] = (grad_normed * xh1[...]).astype(BF16)
    owner = lax.broadcasted_iota(jnp.int32, (384, 256), 0) >> 7
    column = lax.broadcasted_iota(jnp.int32, (384, 256), 1)
    wanted = jnp.where(owner == 2, TAPS, TAPS + 1 + owner)
    sums = tn(prods[...], jnp.where(column == wanted, 1.0, 0.0).astype(BF16))
    parts = [
        sums[128 * k : 128 * k + 128] + tap_grad * jnp.where(group == k, 1.0, 0.0) for k in range(4)
    ]
    split(jnp.concatenate(parts, axis=0), EXT, 256)
    split(tn(nlow[...], grad_val), VAL, 512)
    rs_xe = swap_cores(XE)

    weighted = gain_one * grad_normed
    mean_one = jnp.mean(weighted, axis=1, keepdims=True)
    mean_two = jnp.mean(weighted * xh1[...], axis=1, keepdims=True)
    gin_ref[...] = ghid[...] + (weighted - mean_one - xh1[...] * mean_two) * inv1[...]

    rs_xe = reduce_bulk_x(XE, rs_xe)
    rs_yg = reduce_next_y(YG, rs_yg)
    arrived(rs_d)
    total = accd[:, :, z]
    for k in range(3):
        total = total + r2d[k].astype(F32)
    acc2d[...] = total
    s3d[...] = total.astype(BF16)
    rs_d = ring(y, y_at, lambda to: s3d.at[:, to], lambda i: r3d.at[i - 1])
    reduce_last(XU, rs_xu, y)
    reduce_last(YU, rs_yu, x)
    rs_xe = reduce_next_x(XE, rs_xe)
    reduce_last(YG, rs_yg, x)
    arrived(rs_d)
    total = acc2d[:, y]
    for k in range(3):
        total = total + r3d[k].astype(F32)
    acc3d[...] = total
    s4d[...] = total.astype(BF16)
    rs_d = ring(x, x_at, lambda to: s4d.at[to], lambda i: r4d.at[i - 1])
    reduce_last(XE, rs_xe, y)
    tail[:, END:WIDE] = jnp.zeros((16, WIDE - END), F32)
    stacked = jnp.concatenate(
        [tail[:, 1024 * u : 1024 * u + 1024].astype(BF16) for u in range(4)], axis=0
    )
    s4[...] = nn(swap, stacked).astype(BF16).reshape(4, 16, 1024)
    rs_z = ring(z, z_at, lambda to: s4.at[to], lambda i: r4.at[i - 1])
    arrived(rs_d)
    total = acc3d[x]
    for k in range(3):
        total = total + r4d[k].astype(F32)
    gdown_ref[...] = total
    arrived(rs_z)
    total = s4[z].astype(F32)
    for k in range(3):
        total = total + r4[k].astype(F32)
    gpack_ref[...] = total

    for copy in started:
        if copy is not None:
            copy.wait_send()
    sent_back(sent_c)
    sent_back(sent_g)


def scratch():
    def f32(*shape):
        return pltpu.VMEM(shape, F32)

    def b16(*shape):
        return pltpu.VMEM(shape, BF16)

    copies = 160
    return [
        b16(4, 16, 1024), b16(4, 2, 4, 16, WIDE), b16(4, 2, 4, 4, 16, 512),
        b16(2 * SLOT, SLOT), b16(512, 2 * SLOT), b16(2 * SLOT, 256),
        f32(128, 512), f32(128, 1), b16(128, 512), f32(128, 512), f32(128, 512), f32(128, 512), f32(128, 512),
        b16(128, 512), f32(128, 512), f32(128, 512), b16(128, 512),
        b16(128, 512), f32(128, FF), b16(128, FF), b16(128, FF), f32(128, 512), b16(128, 512), b16(128, 512),
        b16(384, 512),
        b16(8, 64, 128), b16(16, 64, 128), b16(8, 64, 128), b16(8, 64, 128),
        b16(8, 64, 128), b16(16, 64, 128), b16(8, 64, 128), b16(8, 64, 128),
        f32(2 * SLOT, 128), f32(2 * SLOT, 128), f32(2 * SLOT, 128), b16(2 * SLOT, 128),
        f32(4, 4, 16, WIDE), b16(4, 4, 16, WIDE), b16(4, 4, 16, WIDE), b16(4, 4, 16, WIDE), b16(3, 4, 16, WIDE),
        f32(4, 16, WIDE), b16(4, 16, WIDE), b16(3, 16, WIDE), f32(16, WIDE),
        f32(4, 4, 4, 16, 512), b16(4, 4, 4, 16, 512), b16(4, 4, 4, 16, 512), b16(4, 4, 4, 16, 512),
        b16(3, 4, 4, 16, 512), f32(4, 4, 16, 512), b16(4, 4, 16, 512), b16(3, 4, 16, 512),
        f32(4, 16, 512), b16(4, 16, 512), b16(3, 16, 512),
        b16(4, 16, 1024), b16(3, 16, 1024),
        pltpu.SemaphoreType.DMA((copies,)), pltpu.SemaphoreType.DMA((copies,)), pltpu.SemaphoreType.DMA((3,)),
    ]


def body(
    inputs,
    cotangent,
    lengths,
    gain_first,
    proj_in,
    sub_kernels,
    skip_gain,
    proj_out,
    gain_second,
    mlp_up,
    mlp_down,
):
    forward, inverse, repeat = transforms()
    taps = sub_kernels.reshape(TAPS, 4).T
    extras = jnp.concatenate(
        [
            taps,
            gain_first[:, None],
            gain_second[:, None],
            skip_gain[:, None],
            jnp.zeros((4, 256 - TAPS - 3), BF16),
        ],
        axis=1,
    )
    pack = jnp.concatenate(
        [
            proj_in[:, :D],
            extras,
            mlp_up[:, :1024],
            proj_in[:, D:],
            proj_out,
            mlp_up[:, 1024:],
            jnp.zeros((4, WIDE - END), BF16),
        ],
        axis=1,
    )
    pack = pack.reshape(4, 4, 1024).transpose(1, 0, 2).reshape(16, 1024)

    vmem = pl.BlockSpec(memory_space=pltpu.VMEM)
    smem = pl.BlockSpec(memory_space=pltpu.SMEM)
    anywhere = pl.BlockSpec(memory_space=pl.ANY)
    outputs, grad_inputs, gpack, gdown = pl.pallas_call(
        fused,
        out_shape=(
            jax.ShapeDtypeStruct((128, 512), F32),
            jax.ShapeDtypeStruct((128, 512), F32),
            jax.ShapeDtypeStruct((16, 1024), F32),
            jax.ShapeDtypeStruct((16, 512), F32),
        ),
        in_specs=[vmem, vmem, smem, vmem, vmem, anywhere, anywhere, anywhere],
        out_specs=(vmem, vmem, vmem, vmem),
        scratch_shapes=scratch(),
        compiler_params=pltpu.CompilerParams(
            collective_id=0, has_side_effects=True, vmem_limit_bytes=60 * 2**20
        ),
        name="block",
    )(
        inputs.reshape(128, 512),
        cotangent.reshape(128, 512),
        lengths,
        pack,
        mlp_down,
        jnp.asarray(forward),
        jnp.asarray(inverse),
        jnp.asarray(repeat),
    )
    rows = gpack.reshape(4, 4, 1024).transpose(1, 0, 2).reshape(4, WIDE)
    grad_taps = rows[:, EXT : EXT + TAPS]
    share = jnp.asarray(np.repeat(0.5 ** np.arange(NSUB), SUBTAPS).astype(np.float32))[None, :]
    low_taps = taps.astype(F32)
    norm = lax.rsqrt(jnp.sum(low_taps * low_taps * share, axis=1, keepdims=True) + EPSILON)
    along = jnp.sum(low_taps * grad_taps, axis=1, keepdims=True)
    grad_sub = norm * grad_taps - share * low_taps * (norm * norm * norm * along)
    return (
        outputs.reshape(2, 64, 512),
        grad_inputs.reshape(2, 64, 512),
        rows[:, EXT + TAPS],
        jnp.concatenate([rows[:, VAL:EXT], rows[:, GAT:OUT]], axis=1),
        grad_sub.T.reshape(NSUB, SUBTAPS, 4),
        rows[:, EXT + TAPS + 2],
        rows[:, OUT:UPB],
        rows[:, EXT + TAPS + 1],
        jnp.concatenate([rows[:, UPA:GAT], rows[:, UPB:END]], axis=1),
        gdown,
    )


def solution(mesh):
    in_specs = (
        P("dp", "seq", None),
        P("dp", "seq", None),
        P("dp"),
        P(("dp", "seq")),
        P(("dp", "seq"), None),
        P(None, None, ("dp", "seq")),
        P(("dp", "seq")),
        P(("dp", "seq"), None),
        P(("dp", "seq")),
        P(("dp", "seq"), None),
        P(("dp", "seq"), None),
    )
    out_specs = (
        P("dp", "seq", None),
        P("dp", "seq", None),
        P(("dp", "seq")),
        P(("dp", "seq"), None),
        P(None, None, ("dp", "seq")),
        P(("dp", "seq")),
        P(("dp", "seq"), None),
        P(("dp", "seq")),
        P(("dp", "seq"), None),
        P(("dp", "seq"), None),
    )
    return jax.shard_map(body, mesh=mesh, in_specs=in_specs, out_specs=out_specs, check_vma=False)
```

```python
import math

import jax
import jax.numpy as jnp
import ml_dtypes
import numpy as np
from jax import lax
from jax.experimental import pallas as pl
from jax.experimental.pallas import tpu as pltpu
from jax.sharding import PartitionSpec as P

EPSILON = 1e-05
D = 512
FF = 2048
SLOT = 1024
NSUB = 5
SUBTAPS = 32
TAPS = NSUB * SUBTAPS
F32 = jnp.float32
BF16 = jnp.bfloat16
MESH = pl.DeviceIdType.MESH

VAL, EXT, END, UPA, GAT, OUT, UPB, WIDE = 0, 512, 768, 1024, 2048, 2560, 3072, 4096
XE, YE, XR, YR, EARLY = (VAL, 384), (384, END), (UPA, UPB), (UPB, WIDE), (VAL, END)
X1, X2 = (UPA, GAT), (GAT, UPB)
ZD, YD = (0, 384), (384, 512)


def transforms():
    place = np.arange(SLOT)
    angle = 2 * np.pi * ((2 * place[:, None] + 1) * place[None, :] % (4 * SLOT)) / (4 * SLOT)
    forward = np.concatenate([np.cos(angle), -np.sin(angle)], axis=0)
    inverse = forward.T / SLOT
    repeat = np.zeros((SLOT, 256))
    first = 0
    for octave in range(NSUB):
        for tap in range(SUBTAPS):
            repeat[first : first + 2**octave, octave * SUBTAPS + tap] = 0.5**octave
            first += 2**octave
    half = np.stack([inverse[:512], inverse[512:]])
    return tuple(a.astype(ml_dtypes.bfloat16) for a in (forward, half, forward @ repeat))


def nn(a, b):
    return lax.dot_general(a, b, (((1,), (0,)), ((), ())), preferred_element_type=F32)


def nt(a, b):
    return lax.dot_general(a, b, (((1,), (1,)), ((), ())), preferred_element_type=F32)


def tn(a, b):
    return lax.dot_general(a, b, (((0,), (0,)), ((), ())), preferred_element_type=F32)


def gelu_parts(v):
    cdf = 0.5 * (1.0 + lax.erf(v * math.sqrt(0.5)))
    slope = cdf + v * (jnp.exp(-0.5 * v * v) * (1.0 / math.sqrt(2 * math.pi)))
    return v * cdf, slope


def swap_matrix():
    row = lax.broadcasted_iota(jnp.int32, (64, 64), 0)
    col = lax.broadcasted_iota(jnp.int32, (64, 64), 1)
    source = ((row >> 2) & 3) * 16 + (row >> 4) * 4 + (row & 3)
    return jnp.where(col == source, 1.0, 0.0).astype(BF16)


def fused(
    x_hbm, cot_hbm, len_ref, gain_one_hbm, gain_two_hbm, skip_hbm, in_hbm, sub_hbm, mix_hbm, up_hbm, down_hbm,
    dft_hbm, inv_hbm, rep_hbm,
    out_hbm, gin_hbm, gearly_ref, grest_ref, gdown_ref,
    xin, cot, outv, ginv, gain_one_ref, gain_two_ref, skip_ref, in_ref, sub_ref, mix_ref, up_ref, down_ref,
    zearly, zrest, wb, wd, dft, inv, rep,
    xh1, inv1, nlow, val, gated, dgel, mixed, bi, hid, xh2, n2l, gmo, gact, act, gup, ghid, gb, ggate,
    vsend, vin, ysend, cin, gsend, gvin, csend, gcin, nls, nin, spec_v, spec_k, spec_g, spec_y,
    n2t, nlt, bit, act_t, nint,
    acc, csw, crw, s2, r2, acc2, s3, r3, tail,
    accd, csd, crd, s2d, r2a, r2c, acc2a, s3a, r3a, acc2c, s3c, r3c, acc3d, s4d, r4d,
    ta, tcs, tcr, ts2, tr2, tacc, ts3, tr3, s4e, r4e, s4r, r4r,
    send_sem, recv_sem, local_sem,
):
    dp, j = lax.axis_index("dp"), lax.axis_index("seq")
    x, c = dp // 2, dp % 2
    y, z = j // 4, j % 4
    half, pair = j % 2, j // 2
    group = pair % 4

    def turn(v, by):
        return lax.rem(v + by, 4)

    def x_at(v):
        return (v * 2 + c, j)

    def y_at(v):
        return (dp, v * 4 + z)

    def z_at(v):
        return (dp, y * 4 + v)

    sibling = (x * 2 + 1 - c, j)

    barrier = pltpu.get_barrier_semaphore()
    partners = [sibling] + [x_at(turn(x, i)) for i in (1, 2, 3)]
    partners += [(dp, lax.rem(j + i, 16)) for i in range(1, 16)]
    for partner in partners:
        pl.semaphore_signal(barrier, inc=1, device_id=partner, device_id_type=MESH)

    small = [
        pltpu.make_async_copy(src, dst, local_sem.at[8 + k])
        for k, (src, dst) in enumerate((
            (in_hbm, in_ref), (sub_hbm, sub_ref), (gain_one_hbm, gain_one_ref), (gain_two_hbm, gain_two_ref),
            (skip_hbm, skip_ref), (up_hbm, up_ref), (mix_hbm, mix_ref), (down_hbm, down_ref),
        ))
    ]
    loads = [
        pltpu.make_async_copy(x_hbm, xin, local_sem.at[0]),
        pltpu.make_async_copy(cot_hbm, cot, local_sem.at[1]),
        pltpu.make_async_copy(rep_hbm, rep, local_sem.at[2]),
        pltpu.make_async_copy(dft_hbm, dft, local_sem.at[3]),
        pltpu.make_async_copy(inv_hbm.at[half], inv, local_sem.at[4]),
    ]
    for load in small + loads:
        load.start()
    for load in small:
        load.wait()

    lane = lax.broadcasted_iota(jnp.int32, (4, 256), 1)
    extras = jnp.zeros((4, 256), F32)
    for octave in range(NSUB):
        place = lax.broadcasted_iota(jnp.int32, (SUBTAPS, 256), 0) + SUBTAPS * octave
        spread = place == lax.broadcasted_iota(jnp.int32, (SUBTAPS, 256), 1)
        extras = extras + nn(sub_ref[octave], jnp.where(spread, 1.0, 0.0).astype(BF16))
    diagonal = lax.broadcasted_iota(jnp.int32, (4, 4), 0) == lax.broadcasted_iota(jnp.int32, (4, 4), 1)
    for k, ref in enumerate((gain_one_ref, gain_two_ref, skip_ref)):
        column = jnp.sum(jnp.where(diagonal, ref[...].astype(F32), 0.0), axis=1, keepdims=True)
        extras = jnp.where(lane == TAPS + k, column, extras)
    w_in, w_up = in_ref[...].astype(F32), up_ref[...].astype(F32)
    early = [w_in[:, 0:256], w_in[:, 256:512], extras, jnp.zeros((4, 256), F32)]
    zearly[z] = jnp.concatenate(early, axis=0).astype(BF16)
    rest = [
        w_up[:, 0:768],
        jnp.concatenate([w_up[:, 768:1024], w_in[:, 512:1024]], axis=1),
        jnp.concatenate([mix_ref[...].astype(F32), w_up[:, 1024:1280]], axis=1),
        w_up[:, 1280:2048],
    ]
    zrest[z] = jnp.concatenate(rest, axis=0).astype(BF16)
    wd[x, c, y, z] = down_ref[...]
    swap = swap_matrix()

    pl.semaphore_wait(barrier, len(partners))

    started = []

    def push(src, dst, device):
        at = len(started)
        copy = pltpu.make_async_remote_copy(
            src_ref=src,
            dst_ref=dst,
            send_sem=send_sem.at[at],
            recv_sem=recv_sem.at[at],
            device_id=device,
            device_id_type=MESH,
        )
        copy.start()
        started.append(copy)
        return copy

    def ring(me, at, src, dst):
        return [push(src(turn(me, i)), dst(i), at(turn(me, i))) for i in (1, 2, 3)]

    def arrived(copies):
        for copy in copies:
            copy.wait_recv()

    def same(me, at, ref):
        return ring(me, at, lambda to: ref, lambda i: ref)

    def cols(ends):
        return pl.ds(ends[0], ends[1] - ends[0])

    got_z = same(z, z_at, zearly.at[z])
    got_zr = same(z, z_at, zrest.at[z])
    got_d = same(x, x_at, wd.at[x, c, y, z])

    def first_x(p):
        return same(y, y_at, wb.at[x, c, y, :, cols(p)])

    def first_y(p):
        return same(x, x_at, wb.at[x, c, y, :, cols(p)])

    def bulk_x(p):
        return same(x, x_at, wb.at[x, c, :, :, cols(p)])

    def bulk_y(p):
        return same(y, y_at, wb.at[:, c, y, :, cols(p)])

    def to_sibling(p):
        ref = wb.at[:, c, :, :, cols(p)]
        return [push(ref, ref, sibling)]

    arrived(got_z)
    rows = nn(swap, zearly[...].reshape(64, 256)).astype(BF16)
    for q in range(3):
        wb[x, c, y, :, 256 * q : 256 * (q + 1)] = rows[16 * q : 16 * q + 16]
    got_xe, got_ye = first_x(XE), first_y(YE)

    loads[0].wait()
    source = xin[...]
    centered = source - jnp.mean(source, axis=1, keepdims=True)
    inv_one = lax.rsqrt(jnp.mean(centered * centered, axis=1, keepdims=True) + EPSILON)
    inv1[...] = inv_one
    xh1[...] = centered * inv_one

    row = lax.broadcasted_iota(jnp.int32, (128, 1), 0)
    limit = jnp.where(row < 64, len_ref[0], len_ref[1])
    mask = jnp.where((row & 63) + j * 64 < limit, 1.0, 0.0)

    arrived(got_zr)
    rows = nn(swap, zrest[...].reshape(64, 768)).astype(BF16)
    for q in range(4):
        wb[x, c, y, :, UPA + 768 * q : UPA + 768 * (q + 1)] = rows[16 * q : 16 * q + 16]

    arrived(got_xe)
    arrived(got_ye)
    got_xe, got_ye = bulk_x(XE), bulk_y(YE)
    got_xr, got_yr = first_x(XR), first_y(YR)
    arrived(got_d)
    got_zd = same(y, y_at, wd.at[:, c, y, z, :, cols(ZD)])
    got_yd = same(z, z_at, wd.at[:, c, y, z, :, cols(YD)])
    arrived(got_xe)
    arrived(got_ye)
    got_e = to_sibling(EARLY)
    arrived(got_xr)
    got_xr = bulk_x(XR)

    def weight(first, width):
        return wb[:, :, :, :, first : first + width].reshape(512, width)

    arrived(got_e)
    pick = jnp.where(
        lax.broadcasted_iota(jnp.int32, (8, 128), 1)
        == lax.broadcasted_iota(jnp.int32, (8, 128), 0) + (TAPS - 128),
        1.0,
        0.0,
    ).astype(BF16)
    gains = nt(pick, weight(EXT + 128, 128))
    gain_one, gain_two, skip = gains[0:1], gains[1:2], gains[2:3]
    nlow[...] = (xh1[...] * gain_one).astype(BF16)
    nls[...] = nlow[...].reshape(2, 64, 512)
    values = nn(nlow[...], weight(VAL, 512))
    val[...] = values
    low = values.astype(BF16)
    for b in range(2):
        for g in range(4):
            vsend[4 * b + g] = low[64 * b : 64 * b + 64, 128 * g : 128 * g + 128]

    def scatter(src, dst):
        copies = []
        for i in range(1, 16):
            to = lax.rem(j + i, 16)
            copies.append(push(src.at[to // 2], dst.at[j], (dp, to)))
        dst[j] = src[pair]
        return copies

    def eight(src, dst, target, slot, sender, own):
        base = len(started)
        copies, receipts = [], []
        for i in range(8):
            to = target(i)
            copy = pltpu.make_async_remote_copy(
                src_ref=src(i),
                dst_ref=dst.at[slot],
                send_sem=send_sem.at[base + i],
                recv_sem=recv_sem.at[base + slot],
                device_id=(dp, to),
                device_id_type=MESH,
            )

            @pl.when(to != j)
            def _(copy=copy):
                copy.start()

            @pl.when(to == j)
            def _(i=i):
                dst[slot] = own(i)

            copies.append((copy, to))
            started.append(None)
        for i in range(8):
            receipt = pltpu.make_async_remote_copy(
                src_ref=src(i),
                dst_ref=dst.at[i],
                send_sem=send_sem.at[base + i],
                recv_sem=recv_sem.at[base + i],
                device_id=sibling,
                device_id_type=MESH,
            )
            receipts.append((receipt, sender(i)))
        return copies, receipts

    def give_back(src, dst):
        return eight(
            lambda i: src.at[i], dst, lambda i: 8 * half + i, pair, lambda q: 2 * q + j // 8, lambda i: src[i]
        )

    def taken_back(receipts):
        for receipt, sender in receipts:

            @pl.when(sender != j)
            def _(receipt=receipt):
                receipt.wait_recv()

    def sent_back(copies):
        for copy, to in copies:

            @pl.when(to != j)
            def _(copy=copy):
                copy.wait_send()

    got_v = scatter(vsend, vin)
    arrived(got_yr)
    got_yr = bulk_y(YR)
    arrived(got_zd)
    got_zd = same(z, z_at, wd.at[:, c, :, z, :, cols(ZD)])
    arrived(got_yd)
    got_yd = same(y, y_at, wd.at[:, c, y, :, :, cols(YD)])

    taps = wb[group, :, :, :, EXT:END].reshape(128, 256)
    skip_group = nt(pick, taps[:, 128:256])[2:3]
    lane = lax.broadcasted_iota(jnp.int32, (128, 256), 1)
    share = jnp.where(lane < TAPS, 1.0 / (1 << (lane >> 5)).astype(F32), 0.0)
    squares = taps.astype(F32) * taps.astype(F32) * share
    high = squares.astype(BF16)
    rest = (squares - high.astype(F32)).astype(BF16)
    ones = jnp.ones((8, 256), BF16)
    norm = lax.rsqrt((nt(ones, high) + nt(ones, rest))[0:1] + EPSILON)
    loads[2].wait()
    for i in range(4):
        part = pl.ds(512 * i, 512)
        spec_k[part, :] = nt(rep[part, :], taps) * norm

    def spectrum(src, dst):
        signal = src[...].reshape(SLOT, 128)

        def step(i, carry):
            part = pl.ds(pl.multiple_of(i * 256, 256), 256)
            dst[part, :] = nn(dft[part, :], signal)
            return carry

        lax.fori_loop(0, 8, step, 0)

    def back(dst, more=None):
        def step(i, carry):
            part = nn(inv[pl.ds(pl.multiple_of(i * 256, 256), 256), :], spec_y[...])
            if more is not None:
                part = part + more(i)
            dst[pl.ds(i * 4, 4)] = part.astype(BF16).reshape(4, 64, 128)
            return carry

        lax.fori_loop(0, 2, step, 0)

    loads[3].wait()
    loads[4].wait()
    arrived(got_v)
    spectrum(vin, spec_v)
    for i in range(4):
        re, im = pl.ds(256 * i, 256), pl.ds(SLOT + 256 * i, 256)
        kr, ki, vr, vi = spec_k[re, :], spec_k[im, :], spec_v[re, :], spec_v[im, :]
        spec_y[re, :] = (kr * vr - ki * vi).astype(BF16)
        spec_y[im, :] = (kr * vi + ki * vr).astype(BF16)
    back(ysend)
    sent_c, got_c = give_back(ysend, cin)
    sent_n, got_n = eight(
        lambda k: nls.at[k // 4], nin, lambda k: 2 * k + j // 8, j % 8, lambda i: 8 * half + i, lambda k: nls[k // 4]
    )

    arrived(got_xr)
    got_xr = to_sibling(XR)
    arrived(got_yr)
    got_yr = to_sibling(YR)
    arrived(got_zd)
    arrived(got_yd)
    got_dc = [push(wd.at[:, c], wd.at[:, c], sibling)]
    loads[1].wait()
    gmo[...] = (cot[...] * mask).astype(BF16)
    arrived(got_xr)
    gates = nn(nlow[...], weight(GAT, 512))
    gated[...], dgel[...] = gelu_parts(gates)
    arrived(got_yr)
    arrived(got_dc)
    for f in range(4):
        gact[:, 512 * f : 512 * f + 512] = nt(gmo[...], wd[f].reshape(512, 512))

    def whole(ref):
        lines = [jnp.concatenate([ref[4 * b + g] for g in range(4)], axis=1) for b in range(2)]
        return jnp.concatenate(lines, axis=0).astype(F32)

    taken_back(got_c)
    mixed[...] = whole(cin) + skip * val[...]
    bi[...] = (mixed[...] * gated[...]).astype(BF16)
    hidden = xin[...] + mask * nn(bi[...], weight(OUT, 512))
    hid[...] = hidden
    centered = hidden - jnp.mean(hidden, axis=1, keepdims=True)
    inv_two = lax.rsqrt(jnp.mean(centered * centered, axis=1, keepdims=True) + EPSILON)
    xh2[...] = centered * inv_two
    n2l[...] = (xh2[...] * gain_two).astype(BF16)
    up_at = (UPA, UPA + 512, UPB, UPB + 512)
    grad_n2 = jnp.zeros((128, 512), F32)
    for f in range(4):
        part = slice(512 * f, 512 * f + 512)
        w_up = weight(up_at[f], 512)
        gelu, slope = gelu_parts(nn(n2l[...], w_up))
        act[:, part] = gelu.astype(BF16)
        gup[:, part] = (gact[:, part] * slope).astype(BF16)
        grad_n2 = grad_n2 + nt(gup[:, part], w_up)
    weighted = gain_two * grad_n2
    mean_one = jnp.mean(weighted, axis=1, keepdims=True)
    mean_two = jnp.mean(weighted * xh2[...], axis=1, keepdims=True)
    grad_hidden = cot[...] + (weighted - mean_one - xh2[...] * mean_two) * inv_two
    ghid[...] = grad_hidden
    gb[...] = (mask * grad_hidden).astype(BF16)
    grad_bi = nt(gb[...], weight(OUT, 512))
    grad_mixed = grad_bi * gated[...]
    low = grad_mixed.astype(BF16)
    for b in range(2):
        for g in range(4):
            gsend[4 * b + g] = low[64 * b : 64 * b + 64, 128 * g : 128 * g + 128]
    got_g = scatter(gsend, gvin)

    ggate[...] = (grad_bi * mixed[...] * dgel[...]).astype(BF16)
    skip_grad = (grad_mixed * val[...]).astype(BF16)

    def turned(ref):
        return ref[...].astype(F32).T.astype(BF16)

    def grads(lhs, rhs, width, keep, send):
        own, other = lhs[:, c].reshape(-1, 128), lhs[:, 1 - c].reshape(-1, 128)
        for n in range(0, width, 256):
            keep(n, nn(own, rhs(n)))
            send(n, nn(other, rhs(n)).astype(BF16))

    def grads_wide(lhs, rhs, first, width):
        def keep(n, value):
            acc[:, :, :, first + n : first + n + 256] = value.reshape(4, 4, 16, 256)

        def send(n, value):
            csw[:, :, :, first + n : first + n + 256] = value.reshape(4, 4, 16, 256)

        grads(lhs, rhs, width, keep, send)

    def swap_cores(p):
        return [push(csw.at[:, :, :, cols(p)], crw.at[:, :, :, cols(p)], sibling)]

    def add_core(p):
        at = slice(*p)
        for k in range(4):
            total = acc[k, :, :, at] + crw[k, :, :, at].astype(F32)
            acc[k, :, :, at] = total
            s2[k, :, :, at] = total.astype(BF16)

    def reduce_bulk_x(p):
        return ring(
            x, x_at, lambda to: s2.at[to, :, :, cols(p)], lambda i: r2.at[i - 1, :, :, cols(p)]
        )

    def reduce_bulk_y(p):
        return ring(
            y, y_at, lambda to: s2.at[:, to, :, cols(p)], lambda i: r2.at[i - 1, :, :, cols(p)]
        )

    def reduce_next(p, got, own, me, at_device):
        at = slice(*p)
        arrived(got)
        total = own
        for k in range(3):
            total = total + r2[k, :, :, at].astype(F32)
        acc2[:, :, at] = total
        s3[:, :, at] = total.astype(BF16)
        return ring(
            me, at_device, lambda to: s3.at[to, :, cols(p)], lambda i: r3.at[i - 1, :, cols(p)]
        )

    def reduce_next_x(p, got):
        return reduce_next(p, got, acc[x, :, :, slice(*p)], y, y_at)

    def reduce_next_y(p, got):
        return reduce_next(p, got, acc[:, y, :, slice(*p)], x, x_at)

    def reduce_last(p, got, me):
        at = slice(*p)
        arrived(got)
        total = acc2[me, :, at]
        for k in range(3):
            total = total + r3[k, :, at].astype(F32)
        tail[:, at] = total

    def swapped(blocks):
        stacked = jnp.concatenate(blocks, axis=0).astype(BF16)
        return nn(swap, stacked).astype(BF16).reshape(4, 16, -1)

    n2t[...] = turned(n2l).reshape(4, 2, 64, 128)
    grads_wide(n2t, lambda n: gup[:, n : n + 256], UPA, 1024)
    rs_x1 = swap_cores(X1)
    act_t[...] = turned(act).reshape(4, 2, 256, 128)
    for f in range(4):
        for n in range(0, 512, 256):
            part = gmo[:, n : n + 256]
            accd[f, :, :, :, n : n + 256] = nn(act_t[f, c], part).reshape(4, 4, 16, 256)
            other = nn(act_t[f, 1 - c], part).astype(BF16)
            csd[f, :, :, :, n : n + 256] = other.reshape(4, 4, 16, 256)
    rs_d = [push(csd, crd, sibling)]
    arrived(rs_x1)
    add_core(X1)
    rs_x1 = reduce_bulk_x(X1)
    nlt[...] = turned(nlow).reshape(4, 2, 64, 128)
    grads_wide(nlt, lambda n: ggate[:, n : n + 256], GAT, 512)
    bit[...] = turned(bi).reshape(4, 2, 64, 128)
    grads_wide(bit, lambda n: gb[:, n : n + 256], OUT, 512)
    rs_x2 = swap_cores(X2)
    arrived(rs_d)
    for k in range(4):
        total = accd[k] + crd[k].astype(F32)
        accd[k] = total
        s2d[k] = total.astype(BF16)
    rs_zd = ring(
        z, z_at, lambda to: s2d.at[:, :, to, :, cols(ZD)], lambda i: r2a.at[i - 1]
    )
    rs_yd = ring(y, y_at, lambda to: s2d.at[:, to, :, :, cols(YD)], lambda i: r2c.at[i - 1])
    grads_wide(n2t, lambda n: gup[:, 1024 + n : 1280 + n], UPB, 1024)
    rs_yr = swap_cores(YR)
    arrived(rs_x2)
    add_core(X2)
    rs_x2 = reduce_bulk_x(X2)
    arrived(rs_yr)
    add_core(YR)
    rs_yr = reduce_bulk_y(YR)

    taken_back(got_n)
    nint[...] = nin[...].reshape(512, 512).astype(F32).T.astype(BF16).reshape(4, 2, 64, 512)
    arrived(got_g)
    spectrum(gvin, spec_g)
    for i in range(4):
        re, im = pl.ds(256 * i, 256), pl.ds(SLOT + 256 * i, 256)
        kr, ki, gr, gi = spec_k[re, :], spec_k[im, :], spec_g[re, :], spec_g[im, :]
        spec_y[re, :] = (kr * gr + ki * gi).astype(BF16)
        spec_y[im, :] = (kr * gi - ki * gr).astype(BF16)

    def direct(i):
        return skip_group * gvin[pl.ds(8 * half + 4 * i, 4)].reshape(256, 128).astype(F32)

    back(csend, direct)
    sent_g, got_gc = give_back(csend, gcin)

    grad_val = csend[...].reshape(512, 128)
    ta[:, :, :, 0:128] = nn(nint[:, c].reshape(256, 512), grad_val).reshape(4, 4, 16, 128)
    other = nn(nint[:, 1 - c].reshape(256, 512), grad_val).astype(BF16)
    tcs[:, :, :, 0:128] = other.reshape(4, 4, 16, 128)
    re = pl.ds(pl.multiple_of(half * 512, 512), 512)
    im = pl.ds(pl.multiple_of(half * 512 + SLOT, 512), 512)
    vr, vi, gr, gi = spec_v[re, :], spec_v[im, :], spec_g[re, :], spec_g[im, :]
    tap_grad = tn((vr * gr + vi * gi).astype(BF16), rep[re, :])
    tap_grad = (tap_grad + tn((vr * gi - vi * gr).astype(BF16), rep[im, :])) * (1.0 / SLOT)
    column = lax.broadcasted_iota(jnp.int32, (128, 256), 1)
    sums = tn(skip_grad, jnp.where(column == TAPS + 2, 1.0, 0.0).astype(BF16))
    for k in range(4):
        block = sums[128 * k : 128 * k + 128] + tap_grad * jnp.where(group == k, 1.0, 0.0)
        block = block.reshape(2, 4, 16, 256)
        ta[k, :, :, 128:384] = jnp.where(c == 0, block[0], block[1])
        tcs[k, :, :, 128:384] = jnp.where(c == 0, block[1], block[0]).astype(BF16)
    rs_t = [push(tcs, tcr, sibling)]
    arrived(rs_t)
    for k in range(4):
        total = ta[k] + tcr[k].astype(F32)
        ta[k] = total
        ts2[k] = total.astype(BF16)
    rs_t = ring(x, x_at, lambda to: ts2.at[to], lambda i: tr2.at[i - 1])

    mlp_out = jnp.zeros((128, 512), F32)
    for f in range(4):
        mlp_out = mlp_out + nn(act[:, 512 * f : 512 * f + 512], wd[f].reshape(512, 512))
    outv[...] = hid[...] + mask * mlp_out
    stores = [pltpu.make_async_copy(outv, out_hbm, local_sem.at[5])]
    stores[0].start()

    rs_x1 = reduce_next_x(X1, rs_x1)
    arrived(rs_zd)
    total = accd[:, :, z, :, 0:384]
    for k in range(3):
        total = total + r2a[k].astype(F32)
    acc2a[...] = total
    s3a[...] = total.astype(BF16)
    rs_zd = ring(y, y_at, lambda to: s3a.at[:, to], lambda i: r3a.at[i - 1])
    arrived(rs_yd)
    total = accd[:, y, :, :, 384:512]
    for k in range(3):
        total = total + r2c[k].astype(F32)
    acc2c[...] = total
    s3c[...] = total.astype(BF16)
    rs_yd = ring(z, z_at, lambda to: s3c.at[:, to], lambda i: r3c.at[i - 1])
    rs_yr = reduce_next_y(YR, rs_yr)
    rs_x2 = reduce_next_x(X2, rs_x2)
    arrived(rs_t)
    total = ta[x]
    for k in range(3):
        total = total + tr2[k].astype(F32)
    tacc[...] = total
    ts3[...] = total.astype(BF16)
    rs_t = ring(y, y_at, lambda to: ts3.at[to], lambda i: tr3.at[i - 1])

    taken_back(got_gc)
    grad_val = whole(gcin).astype(BF16)
    weighted = gain_one * (nt(grad_val, weight(VAL, 512)) + nt(ggate[...], weight(GAT, 512)))
    mean_one = jnp.mean(weighted, axis=1, keepdims=True)
    mean_two = jnp.mean(weighted * xh1[...], axis=1, keepdims=True)
    ginv[...] = ghid[...] + (weighted - mean_one - xh1[...] * mean_two) * inv1[...]
    stores.append(pltpu.make_async_copy(ginv, gin_hbm, local_sem.at[6]))
    stores[1].start()

    arrived(rs_zd)
    arrived(rs_yd)
    total = acc2a[:, y]
    for k in range(3):
        total = total + r3a[k].astype(F32)
    acc3d[:, :, 0:384] = total
    s4d[:, :, 0:384] = total.astype(BF16)
    total = acc2c[:, z]
    for k in range(3):
        total = total + r3c[k].astype(F32)
    acc3d[:, :, 384:512] = total
    s4d[:, :, 384:512] = total.astype(BF16)
    rs_d = ring(x, x_at, lambda to: s4d.at[to], lambda i: r4d.at[i - 1])
    reduce_last(X1, rs_x1, y)
    reduce_last(YR, rs_yr, x)
    reduce_last(X2, rs_x2, y)
    s4r[...] = swapped([tail[:, UPA + 768 * q : UPA + 768 * (q + 1)] for q in range(4)])
    rs_z = ring(z, z_at, lambda to: s4r.at[to], lambda i: r4r.at[i - 1])
    arrived(rs_t)
    own, far = tacc[y], tr3[1].astype(F32)
    near = tr3[0].astype(F32) + tr3[2].astype(F32)
    even = y % 2 == 0
    same_group, other_group = own[:, 0:128] + far[:, 0:128], near[:, 0:128]
    extras = own[:, 128:384] + far[:, 128:384] + near[:, 128:384]
    s4e[...] = swapped(
        [
            jnp.where(even, same_group, other_group),
            jnp.where(even, other_group, same_group),
            extras[:, 0:128],
            extras[:, 128:256],
        ]
    )
    rs_t = ring(z, z_at, lambda to: s4e.at[to], lambda i: r4e.at[i - 1])
    arrived(rs_d)
    total = acc3d[x]
    for k in range(3):
        total = total + r4d[k].astype(F32)
    gdown_ref[...] = total
    arrived(rs_z)
    total = s4r[z].astype(F32)
    for k in range(3):
        total = total + r4r[k].astype(F32)
    grest_ref[...] = total
    arrived(rs_t)
    value_low, value_high, extras = jnp.zeros((8, 128), F32), jnp.zeros((8, 128), F32), jnp.zeros((8, 128), F32)
    for k in range(4):
        block = (s4e[z] if k == 0 else r4e[k - 1]).astype(F32)
        is_low = jnp.where(turn(z, 4 - k) < 2, 1.0, 0.0)
        value_low = value_low + block[0:8] * is_low
        value_high = value_high + block[0:8] * (1.0 - is_low)
        extras = extras + block[8:16]
    gearly_ref[0:8] = value_low
    gearly_ref[8:16] = value_high
    gearly_ref[16:24] = extras

    for store in stores:
        store.wait()
    for copy in started:
        if copy is not None:
            copy.wait_send()
    sent_back(sent_c)
    sent_back(sent_n)
    sent_back(sent_g)


def scratch():
    def f32(*shape):
        return pltpu.VMEM(shape, F32)

    def b16(*shape):
        return pltpu.VMEM(shape, BF16)

    copies = 192
    return [
        f32(128, 512), f32(128, 512), f32(128, 512), f32(128, 512),
        b16(1, 4), b16(1, 4), b16(1, 4), b16(4, 1024), b16(NSUB, 4, SUBTAPS), b16(4, 512), b16(4, 2048), b16(16, 512),
        b16(4, 16, 256), b16(4, 16, 768), b16(4, 2, 4, 16, WIDE), b16(4, 2, 4, 4, 16, 512),
        b16(2 * SLOT, SLOT), b16(512, 2 * SLOT), b16(2 * SLOT, 256),
        f32(128, 512), f32(128, 1), b16(128, 512), f32(128, 512), f32(128, 512), f32(128, 512), f32(128, 512),
        b16(128, 512), f32(128, 512), f32(128, 512), b16(128, 512),
        b16(128, 512), f32(128, FF), b16(128, FF), b16(128, FF), f32(128, 512), b16(128, 512), b16(128, 512),
        b16(8, 64, 128), b16(16, 64, 128), b16(8, 64, 128), b16(8, 64, 128),
        b16(8, 64, 128), b16(16, 64, 128), b16(8, 64, 128), b16(8, 64, 128), b16(2, 64, 512), b16(8, 64, 512),
        f32(2 * SLOT, 128), f32(2 * SLOT, 128), f32(2 * SLOT, 128), b16(2 * SLOT, 128),
        b16(4, 2, 64, 128), b16(4, 2, 64, 128), b16(4, 2, 64, 128), b16(4, 2, 256, 128), b16(4, 2, 64, 512),
        f32(4, 4, 16, WIDE), b16(4, 4, 16, WIDE), b16(4, 4, 16, WIDE), b16(4, 4, 16, WIDE), b16(3, 4, 16, WIDE),
        f32(4, 16, WIDE), b16(4, 16, WIDE), b16(3, 16, WIDE), f32(16, WIDE),
        f32(4, 4, 4, 16, 512), b16(4, 4, 4, 16, 512), b16(4, 4, 4, 16, 512), b16(4, 4, 4, 16, 512),
        b16(3, 4, 4, 16, 384), b16(3, 4, 4, 16, 128),
        f32(4, 4, 16, 384), b16(4, 4, 16, 384), b16(3, 4, 16, 384),
        f32(4, 4, 16, 128), b16(4, 4, 16, 128), b16(3, 4, 16, 128),
        f32(4, 16, 512), b16(4, 16, 512), b16(3, 16, 512),
        f32(4, 4, 16, 384), b16(4, 4, 16, 384), b16(4, 4, 16, 384), b16(4, 4, 16, 384), b16(3, 4, 16, 384),
        f32(4, 16, 384), b16(4, 16, 384), b16(3, 16, 384),
        b16(4, 16, 128), b16(3, 16, 128), b16(4, 16, 768), b16(3, 16, 768),
        pltpu.SemaphoreType.DMA((copies,)), pltpu.SemaphoreType.DMA((copies,)), pltpu.SemaphoreType.DMA((16,)),
    ]


def finish(
    out_raw, gin_raw, early_ref, rest_ref, down_raw, sub_ref, w_in_ref, w_up_ref, gain_one_ref, gain_two_ref,
    out_ref, gin_ref, one_ref, in_ref, gsub_ref, skip_ref, mix_ref, two_ref, up_ref, down_ref,
):
    out_ref[...] = out_raw[...]
    gin_ref[...] = gin_raw[...]
    for block, row in enumerate((0, 8, 4, 12)):
        in_ref[:, 128 * block : 128 * (block + 1)] = early_ref[row : row + 4]
    in_ref[:, 512:1024] = rest_ref[4:8, 256:768]
    up_ref[:, 0:768] = rest_ref[0:4]
    up_ref[:, 768:1024] = rest_ref[4:8, 0:256]
    up_ref[:, 1024:1280] = rest_ref[8:12, 512:768]
    up_ref[:, 1280:2048] = rest_ref[12:16]
    mix_ref[...] = rest_ref[8:12, 0:512]
    down_ref[...] = down_raw[...]
    extras = jnp.concatenate([early_ref[16:20], early_ref[20:24]], axis=1)
    diagonal = lax.broadcasted_iota(jnp.int32, (4, 4), 0) == lax.broadcasted_iota(jnp.int32, (4, 4), 1)
    lane = lax.broadcasted_iota(jnp.int32, (4, 256), 1)

    def as_row(column):
        return jnp.sum(jnp.where(diagonal, column, 0.0), axis=0, keepdims=True)

    skip_ref[...] = as_row(jnp.sum(jnp.where(lane == TAPS + 2, extras, 0.0), axis=1, keepdims=True))
    for ref, gain, weight, grad in (
        (one_ref, gain_one_ref, w_in_ref, in_ref),
        (two_ref, gain_two_ref, w_up_ref, up_ref),
    ):
        along = jnp.sum(weight[...].astype(F32) * grad[...], axis=1, keepdims=True)
        ref[...] = as_row(along) / gain[...].astype(F32)
    taps = [sub_ref[i].astype(F32) for i in range(NSUB)]
    grads = [extras[:, SUBTAPS * i : SUBTAPS * (i + 1)] for i in range(NSUB)]
    squares, along = jnp.zeros((4, SUBTAPS), F32), jnp.zeros((4, SUBTAPS), F32)
    for i in range(NSUB):
        squares = squares + taps[i] * taps[i] * 0.5**i
        along = along + taps[i] * grads[i]
    norm = lax.rsqrt(jnp.sum(squares, axis=1, keepdims=True) + EPSILON)
    pull = norm * norm * norm * jnp.sum(along, axis=1, keepdims=True)
    for i in range(NSUB):
        gsub_ref[i] = norm * grads[i] - 0.5**i * taps[i] * pull


def body(
    inputs,
    cotangent,
    lengths,
    gain_first,
    proj_in,
    sub_kernels,
    skip_gain,
    proj_out,
    gain_second,
    mlp_up,
    mlp_down,
):
    forward, inverse, repeat = transforms()
    taps = sub_kernels.transpose(0, 2, 1)
    vmem = pl.BlockSpec(memory_space=pltpu.VMEM)
    smem = pl.BlockSpec(memory_space=pltpu.SMEM)
    anywhere = pl.BlockSpec(memory_space=pl.ANY)

    def f32(*shape):
        return jax.ShapeDtypeStruct(shape, F32)

    outputs, grad_inputs, early, rest, down = pl.pallas_call(
        fused,
        out_shape=(f32(128, 512), f32(128, 512), f32(24, 128), f32(16, 768), f32(16, 512)),
        in_specs=[anywhere, anywhere, smem] + [anywhere] * 11,
        out_specs=(anywhere, anywhere, vmem, vmem, vmem),
        scratch_shapes=scratch(),
        compiler_params=pltpu.CompilerParams(
            collective_id=0, has_side_effects=True, vmem_limit_bytes=60 * 2**20
        ),
        name="block",
    )(
        inputs.reshape(128, 512),
        cotangent.reshape(128, 512),
        lengths,
        gain_first.reshape(1, 4),
        gain_second.reshape(1, 4),
        skip_gain.reshape(1, 4),
        proj_in,
        taps,
        proj_out,
        mlp_up,
        mlp_down,
        jnp.asarray(forward),
        jnp.asarray(inverse),
        jnp.asarray(repeat),
    )
    outputs, grad_inputs, one, w_in, g_sub, skip, w_out, two, up, down = pl.pallas_call(
        finish,
        out_shape=(
            f32(128, 512), f32(128, 512), f32(1, 4), f32(4, 1024), f32(NSUB, 4, SUBTAPS), f32(1, 4),
            f32(4, 512), f32(1, 4), f32(4, 2048), f32(16, 512),
        ),
        in_specs=[vmem] * 10,
        out_specs=(vmem,) * 10,
        name="finish",
    )(
        outputs, grad_inputs, early, rest, down, taps, proj_in, mlp_up,
        gain_first.reshape(1, 4), gain_second.reshape(1, 4),
    )
    return (
        outputs.reshape(2, 64, 512),
        grad_inputs.reshape(2, 64, 512),
        one.reshape(4),
        w_in,
        g_sub.transpose(0, 2, 1),
        skip.reshape(4),
        w_out,
        two.reshape(4),
        up,
        down,
    )


def solution(mesh):
    in_specs = (
        P("dp", "seq", None),
        P("dp", "seq", None),
        P("dp"),
        P(("dp", "seq")),
        P(("dp", "seq"), None),
        P(None, None, ("dp", "seq")),
        P(("dp", "seq")),
        P(("dp", "seq"), None),
        P(("dp", "seq")),
        P(("dp", "seq"), None),
        P(("dp", "seq"), None),
    )
    out_specs = (
        P("dp", "seq", None),
        P("dp", "seq", None),
        P(("dp", "seq")),
        P(("dp", "seq"), None),
        P(None, None, ("dp", "seq")),
        P(("dp", "seq")),
        P(("dp", "seq"), None),
        P(("dp", "seq")),
        P(("dp", "seq"), None),
        P(("dp", "seq"), None),
    )
    return jax.shard_map(body, mesh=mesh, in_specs=in_specs, out_specs=out_specs, check_vma=False)
```
